32 devices in a mesh: wave: 8 (over y, x, core), pole: 4 (over z).
Axes of the slice: x: 2, y: 2, z: 4, core: 2. Of those that a mesh axis runs over, the one named last changes fastest.
Arguments:
- grid: float32 [6, 128, 3072], P(None, None, 'wave'), may hold values from -6 to 6
- legendre: bfloat16 [128, 2, 1536, 1024], P('wave', None, None, 'pole'), may hold values from -0.15625 to 0.15625
- wave_table: int32 [128], replicated, may hold values from 0 to 127, each once
- pole_table: float32 [4, 32], replicated, may hold values from -1.5 to 2.5, as said below
- pole_index: int32 [16], replicated, may hold values from 0 to 31
Outputs:
- next_state: float32 [6, 2, 128, 1024], P(None, None, 'wave', 'pole')
The draws below stay inside these ranges and needn't reach their ends.
Inputs may be any that keep to these rules, and one draw needn't show every extreme that they name: Slot s holds zonal wavenumber wave_table[s], every wavenumber of 0 to 127 once; row s of legendre belongs to it. `pole_table`: shift real parts lie in 1.5 to 2.5, shift imaginary parts in -1.5 to 1.5, weights in -1.2 to 1.2.
All inputs are finite; a program needn't handle non-finite values.
Results may differ from the reference program's by a relative error of at most 0.0003.
Values sent between devices are 32-bit elements; how exact they have to be, the bound alone decides.
A program may use at most 128 MiB of HBM per device.

```python
import jax
import jax.numpy as jnp
from jax import lax

NLAT = 3072
NHALF = 1536
NDEG_PAR = 1024
M_ALL = 128
NSOLVE = 16
NTABLE = 32
SWEEPS = 8


def draw_pole_table(key, part):
    first, second, third, fourth = jax.random.split(key, 4)
    ushift = jax.random.uniform(first, (NTABLE,), jnp.float32)
    vshift = jax.random.uniform(second, (NTABLE,), jnp.float32)
    shift_re = 1.5 + ushift
    shift_im = 3.0 * vshift - 1.5
    weight_re = jnp.clip(0.3 * jax.random.normal(third, (NTABLE,), jnp.float32), -1.2, 1.2)
    weight_im = jnp.clip(0.3 * jax.random.normal(fourth, (NTABLE,), jnp.float32), -1.2, 1.2)
    return jnp.stack([shift_re, shift_im, weight_re, weight_im]).astype(jnp.float32)


def touch_ends(entries, stream_key, least, high):
    spot = [jax.random.randint(jax.random.fold_in(stream_key, axis), (), 0, length) for axis, length in enumerate(entries.shape)]
    widest = entries.shape.index(max(entries.shape))
    neighbour = spot[:widest] + [(spot[widest] + 1) % entries.shape[widest]] + spot[widest + 1:]
    return entries.at[tuple(spot)].set(least).at[tuple(neighbour)].set(high)


def block_levels(own_key, dims, cuts, least, top_value):
    gain, own = 1.0, jax.random.fold_in(own_key, 6)
    for dim, blocks in cuts:
        heights = jnp.exp(jax.random.uniform(jax.random.fold_in(own, dim), (blocks,), jnp.float32, least / len(cuts), top_value / len(cuts)))
        gain = gain * jnp.repeat(heights, dims[dim] // blocks).reshape([-1 if axis == dim else 1 for axis in range(len(dims))])
    return gain


def bell_draw(key, dims, deviation, most, pieces=(), held_as=jnp.bfloat16):
    level = block_levels(key, dims, pieces, -0.22, 0.18) if pieces else 1.0
    array = jax.random.normal(key, dims, jnp.float32) * deviation * level
    return jnp.minimum(jnp.maximum(array, -most), most).astype(held_as)


def setup_inputs(seed: int = 0) -> dict:
    splits = jax.random.split(jax.random.key(seed), 6)
    return {
        "grid": bell_draw(splits[0], (6, M_ALL, NLAT), 1.0, 6.0, ((2, 8),), jnp.float32),
        "legendre": bell_draw(splits[1], (M_ALL, 2, NHALF, NDEG_PAR), NHALF ** -0.5, 0.15625, ((0, 8), (3, 4))),
        "wave_table": jax.random.permutation(splits[2], M_ALL).astype(jnp.int32),
        "pole_table": draw_pole_table(jax.random.fold_in(splits[5], 71), 0),
        "pole_index": touch_ends(jax.random.randint(splits[4], (NSOLVE,), 0, NTABLE), jax.random.fold_in(splits[4], 1), 0, NTABLE - 1).astype(jnp.int32),
    }


coriolis_step = 1.2
gravity_step = 0.0008

def split_high(values):
    upper_part = values.astype(jnp.bfloat16)
    kept = lax.optimization_barrier(upper_part)
    lower_part = (values - kept.astype(jnp.float32)).astype(jnp.bfloat16)
    return (upper_part, lower_part)

def coefficients(wavenum, start, count):
    index = (start + jnp.arange(count, dtype=jnp.int32)).astype(jnp.float32)
    parity = jnp.arange(2, dtype=jnp.int32).astype(jnp.float32)
    order = (2.0 * index[None, :] + parity[:, None])[:, None, :]
    wave = wavenum[None, :, None]
    degree = wave + order
    product = degree * (degree + 1.0)
    rossby = coriolis_step * wave / jnp.maximum(product, 2.0)
    gravity = gravity_step * jnp.sqrt(product)
    e_lo = jnp.sqrt(order * (2.0 * wave + order) / jnp.maximum(4.0 * degree * degree - 1.0, 1.0))
    after = order + 1.0
    upper_deg = degree + 1.0
    e_hi = jnp.sqrt(after * (2.0 * wave + after) / jnp.maximum(4.0 * upper_deg * upper_deg - 1.0, 1.0))
    return (e_lo, e_hi, rossby, gravity)

def cmul(are, aim, bre, bim):
    return (are * bre - aim * bim, are * bim + aim * bre)

def zero_extend(field):
    return jnp.pad(field, ((0, 0), (0, 0), (0, 0), (0, 0), (1, 1)))

def solve(spectra, coef, shifts, extend):
    e_lo, e_hi, rossby, gravity = coef
    count = spectra.shape[3]
    shift_re = shifts[:, 0][:, None, None, None]
    shift_im = shifts[:, 1][:, None, None, None]
    weight_re = shifts[:, 2][:, None, None, None]
    weight_im = shifts[:, 3][:, None, None, None]
    z0r, z0i = (spectra[0][None], spectra[1][None])
    d0r, d0i = (spectra[2][None], spectra[3][None])
    h0r, h0i = (spectra[4][None], spectra[5][None])
    b_re = shift_re + 0.0 * rossby[None]
    b_im = shift_im + rossby[None]
    b_mag = b_re * b_re + b_im * b_im
    inv_re, inv_im = (b_re / b_mag, -b_im / b_mag)
    det_re, det_im = cmul(b_re, b_im, shift_re, shift_im)
    det_re = det_re + gravity[None] * gravity[None]
    det_mag = det_re * det_re + det_im * det_im
    dinv_re, dinv_im = (det_re / det_mag, -det_im / det_mag)
    grav = gravity[None]
    hb_re, hb_im = cmul(b_re, b_im, h0r, h0i)
    zr, zi, dr, di, hr, hi = (z0r, z0i, d0r, d0i, h0r, h0i)
    for sweep in range(SWEEPS):
        if sweep == 0:
            rzr, rzi, rdr, rdi = (z0r, z0i, d0r, d0i)
        else:
            both = jnp.stack([zr, zi, dr, di], axis=0)
            ext = extend(both)
            lower = jnp.stack([ext[:, :, 1, :, 0:count], ext[:, :, 0, :, 1:count + 1]], axis=2)
            upper = jnp.stack([ext[:, :, 1, :, 1:count + 1], ext[:, :, 0, :, 2:count + 2]], axis=2)
            near = e_lo * lower + e_hi * upper
            rzr = z0r - coriolis_step * near[2]
            rzi = z0i - coriolis_step * near[3]
            rdr = d0r + coriolis_step * near[0]
            rdi = d0i + coriolis_step * near[1]
        zr, zi = cmul(rzr, rzi, inv_re, inv_im)
        nd_re, nd_im = cmul(shift_re, shift_im, rdr, rdi)
        nd_re = nd_re + grav * h0r
        nd_im = nd_im + grav * h0i
        nh_re = hb_re - grav * rdr
        nh_im = hb_im - grav * rdi
        dr, di = cmul(nd_re, nd_im, dinv_re, dinv_im)
        hr, hi = cmul(nh_re, nh_im, dinv_re, dinv_im)
    parts = []
    for field_re, field_im in ((zr, zi), (dr, di), (hr, hi)):
        out_re, out_im = cmul(weight_re, weight_im, field_re, field_im)
        parts.append(lax.optimization_barrier(jnp.sum(out_re, axis=0)))
        parts.append(lax.optimization_barrier(jnp.sum(out_im, axis=0)))
    return jnp.stack(parts, axis=0)

def reference(grid, legendre, wave_table, pole_table, pole_index):
    columns = jnp.take(grid, wave_table, axis=1)
    half = columns.shape[2] // 2
    north = columns[:, :, :half]
    south = columns[:, :, half:]
    parts = jnp.stack([north + south, north - south], axis=1)
    high, low = split_high(parts)
    high_slots = jnp.moveaxis(high, 2, 0)
    low_slots = jnp.moveaxis(low, 2, 0)

    def analyse_one(trio):
        leg_one, high_one, low_one = trio
        leg_wide = leg_one.astype(jnp.float32)
        first = jnp.einsum('plk,cpl->cpk', leg_wide, high_one.astype(jnp.float32), precision=lax.Precision.HIGHEST)
        second = jnp.einsum('plk,cpl->cpk', leg_wide, low_one.astype(jnp.float32), precision=lax.Precision.HIGHEST)
        return first + second
    out = lax.map(analyse_one, (legendre, high_slots, low_slots))
    spectra = jnp.transpose(out, (1, 2, 0, 3))
    coef = coefficients(wave_table.astype(jnp.float32), 0, spectra.shape[3])
    shifts = jnp.transpose(pole_table[:, pole_index])

    def accumulate(total, row):
        return (total + solve(spectra, coef, row[None], zero_extend), None)
    total, unused = lax.scan(accumulate, jnp.zeros(spectra.shape, jnp.float32), shifts)
    return total
```

```python
import functools

import jax
import jax.numpy as jnp
from jax import lax
from jax.experimental import pallas as pl
from jax.experimental.pallas import tpu as pltpu
from jax.sharding import PartitionSpec as P

SWEEPS = 8
GROUP = 8
HALO = 4
LANES = 128
MESH = pl.DeviceIdType.MESH

coriolis_step = 1.2
gravity_step = 0.0008


def cmul(are, aim, bre, bim):
    return (are * bre - aim * bim, are * bim + aim * bre)


def coefficients(wave, position, valid, parity):
    order = 2.0 * position + parity
    degree = wave + order
    product = degree * (degree + 1.0)
    rossby = coriolis_step * wave / jnp.maximum(product, 2.0)
    gravity = gravity_step * jnp.sqrt(product)
    e_lo = jnp.sqrt(order * (2.0 * wave + order) / jnp.maximum(4.0 * degree * degree - 1.0, 1.0))
    after = order + 1.0
    upper_deg = degree + 1.0
    e_hi = jnp.sqrt(
        after * (2.0 * wave + after) / jnp.maximum(4.0 * upper_deg * upper_deg - 1.0, 1.0)
    )
    e_lo = jnp.where(valid, coriolis_step * e_lo, 0.0)
    e_hi = jnp.where(valid, coriolis_step * e_hi, 0.0)
    return e_lo, e_hi, rossby, gravity


def kernel(
    waves,
    poles,
    grid_hbm,
    leg_hbm,
    wave_table,
    pole_table,
    pole_index,
    out_ref,
    grid_v,
    leg_v,
    send,
    recv,
    parts,
    spec,
    coef,
    halo_send,
    halo_recv,
    grid_sem,
    leg_sem,
    send_sem,
    recv_sem,
    halo_send_sem,
    halo_recv_sem,
):
    comps = grid_hbm.shape[0]
    lat = grid_hbm.shape[2]
    slots = leg_hbm.shape[0]
    count = leg_hbm.shape[3]
    groups = slots // GROUP
    half = waves // 2
    rows = GROUP * comps
    width = count + LANES
    solves = pole_index.shape[0]
    me = lax.axis_index("wave")
    zone = lax.axis_index("pole")

    barrier = pltpu.get_barrier_semaphore()
    for step in range(1, waves):
        pl.semaphore_signal(
            barrier, inc=1, device_id=(lax.rem(me + step, waves), zone), device_id_type=MESH
        )

    @pl.when(zone > 0)
    def _():
        pl.semaphore_signal(barrier, inc=1, device_id=(me, zone - 1), device_id_type=MESH)

    @pl.when(zone < poles - 1)
    def _():
        pl.semaphore_signal(barrier, inc=1, device_id=(me, zone + 1), device_id_type=MESH)

    grid_copy = pltpu.make_async_copy(grid_hbm, grid_v, grid_sem)
    grid_copy.start()
    leg_copies = [
        pltpu.make_async_copy(leg_hbm.at[s], leg_v.at[s], leg_sem.at[s]) for s in range(slots)
    ]
    for copy in leg_copies:
        copy.start()
    parts[:, :, rows:, :] = jnp.zeros((half, 2, parts.shape[2] - rows, lat), jnp.float32)
    grid_copy.wait()

    def collect(target, g, d):
        for s in range(GROUP):
            m = wave_table[d * slots + g * GROUP + s]
            for c in range(comps):
                target[g, d, s * comps + c : s * comps + c + 1, :] = grid_v[c, pl.ds(m, 1), :]

    def exchange(g, there, here):
        return pltpu.make_async_remote_copy(
            src_ref=send.at[g, there],
            dst_ref=recv.at[g, here],
            send_sem=send_sem.at[g, there],
            recv_sem=recv_sem.at[g, here],
            device_id=(there, zone),
            device_id_type=MESH,
        )

    neighbours = (zone > 0).astype(jnp.int32) + (zone < poles - 1).astype(jnp.int32)
    pl.semaphore_wait(barrier, waves - 1 + neighbours)

    for g in range(groups):

        def send_one(step, carry, g=g):
            there = lax.rem(me + step, waves)
            collect(send, g, there)
            exchange(g, there, me).start()
            return carry

        lax.fori_loop(1, waves, send_one, 0)
    for g in range(groups):
        collect(recv, g, me)

    lane = lax.broadcasted_iota(jnp.int32, (GROUP, LANES), 1)
    line = lax.broadcasted_iota(jnp.int32, (GROUP, width), 0)
    place = lax.broadcasted_iota(jnp.int32, (GROUP, width), 1)
    local = jnp.where(place >= width - HALO, place - width, place)
    k_index = local + zone * count
    valid = (local < count + HALO) & (k_index >= 0) & (k_index < poles * count)
    position = k_index.astype(jnp.float32)

    def left_copy(g):
        return pltpu.make_async_remote_copy(
            src_ref=halo_send.at[g, 0],
            dst_ref=halo_recv.at[g, 1],
            send_sem=halo_send_sem.at[g, 0],
            recv_sem=halo_recv_sem.at[g, 1],
            device_id=(me, lax.rem(zone + poles - 1, poles)),
            device_id_type=MESH,
        )

    def right_copy(g):
        return pltpu.make_async_remote_copy(
            src_ref=halo_send.at[g, 1],
            dst_ref=halo_recv.at[g, 0],
            send_sem=halo_send_sem.at[g, 1],
            recv_sem=halo_recv_sem.at[g, 0],
            device_id=(me, lax.rem(zone + 1, poles)),
            device_id_type=MESH,
        )

    def group_step(g, carry):
        wave = jnp.zeros((GROUP, width), jnp.float32)
        for s in range(GROUP):
            m = wave_table[me * slots + g * GROUP + s].astype(jnp.float32)
            wave = jnp.where(line == s, m, wave)
        for p in range(2):
            for i, value in enumerate(coefficients(wave, position, valid, float(p))):
                coef[i, p] = value

        for w in range(half):
            for source in (w, w + half):

                @pl.when(me != source)
                def _():
                    exchange(g, source, source).wait_recv()

            north = recv[g, w]
            south = recv[g, w + half]
            parts[w, 0, 0:rows, :] = north + south
            parts[w, 1, 0:rows, :] = north - south

        span = half if lat % LANES == 0 else 1
        for s in range(GROUP):
            slot = g * GROUP + s
            pltpu.make_async_copy(leg_hbm.at[slot], leg_v.at[slot], leg_sem.at[slot]).wait()

            def analyse(p, carry, s=s, slot=slot):
                total = jnp.zeros((16, count), jnp.float32)
                for first in range(0, half, span):
                    pieces = []
                    for w in range(first, first + span):
                        value = parts[w, p, s * comps : s * comps + 8, :]
                        high = value.astype(jnp.bfloat16).astype(jnp.float32)
                        pieces.append(jnp.concatenate([high, value - high], axis=0))
                    left = jnp.concatenate(pieces, axis=1) if span > 1 else pieces[0]
                    total = total + jnp.dot(
                        left.astype(jnp.bfloat16),
                        leg_v[slot, p, first * lat : (first + span) * lat, :],
                        preferred_element_type=jnp.float32,
                    )
                both = total[0:8] + total[8:16]
                for c in range(comps):
                    spec[c, p, s : s + 1, 0:count] = both[c : c + 1]
                return carry

            lax.fori_loop(0, 2, analyse, 0)

        lower = jnp.zeros((GROUP, LANES), jnp.float32)
        upper = jnp.zeros((GROUP, LANES), jnp.float32)
        for i in range(2 * comps):
            c, p = i // 2, i % 2
            mine = (lane >= HALO * i) & (lane < HALO * (i + 1))
            first = spec[c, p, :, 0:LANES]
            last = spec[c, p, :, count - LANES : count]
            lower = jnp.where(mine, pltpu.roll(first, HALO * i, 1) if i else first, lower)
            upper = jnp.where(mine, pltpu.roll(last, HALO * (i + 1), 1), upper)
        halo_send[g, 0] = lower
        halo_send[g, 1] = upper

        @pl.when(zone > 0)
        def _():
            left_copy(g).start()

        @pl.when(zone < poles - 1)
        def _():
            right_copy(g).start()

        @pl.when(zone > 0)
        def _():
            right_copy(g).wait_recv()
            left_copy(g).wait_send()

        @pl.when(zone < poles - 1)
        def _():
            left_copy(g).wait_recv()
            right_copy(g).wait_send()

        from_left = halo_recv[g, 0]
        from_right = halo_recv[g, 1]
        for i in range(2 * comps):
            c, p = i // 2, i % 2
            right = pltpu.roll(from_right, LANES - HALO * i, 1) if i else from_right
            left = pltpu.roll(from_left, LANES - HALO * (i + 1), 1)
            edge = jnp.where((lane < HALO) & (zone < poles - 1), right, 0.0)
            edge = jnp.where((lane >= LANES - HALO) & (zone > 0), left, edge)
            spec[c, p, :, count:width] = edge

        home = pl.ds(pl.multiple_of(g * GROUP, GROUP), GROUP)
        out_ref[:, :, home, :] = jnp.zeros((comps, 2, GROUP, count), jnp.float32)

        def near(field):
            even, odd = field
            first = coef[0, 0] * pltpu.roll(odd, 1, 1) + coef[1, 0] * odd
            second = coef[0, 1] * even + coef[1, 1] * pltpu.roll(even, width - 1, 1)
            return first, second

        def pole_step(q, carry):
            column = pole_index[q]
            a_re, a_im = pole_table[0, column], pole_table[1, column]
            w_re, w_im = pole_table[2, column], pole_table[3, column]
            inv, turn, z_first, d_first, dinv, b_all = [], [], [], [], [], []
            for p in range(2):
                rossby, grav = coef[2, p], coef[3, p]
                b_re = a_re + 0.0 * rossby
                b_im = a_im + rossby
                b_mag = 1.0 / (b_re * b_re + b_im * b_im)
                i_re, i_im = b_re * b_mag, -b_im * b_mag
                det_re, det_im = cmul(b_re, b_im, a_re, a_im)
                det_re = det_re + grav * grav
                det_mag = 1.0 / (det_re * det_re + det_im * det_im)
                v_re, v_im = det_re * det_mag, -det_im * det_mag
                t_re, t_im = cmul(a_re, a_im, v_re, v_im)
                g_re, g_im = cmul(v_re, v_im, grav * spec[4, p], grav * spec[5, p])
                d_re, d_im = cmul(t_re, t_im, spec[2, p], spec[3, p])
                inv.append((i_re, i_im))
                turn.append((t_re, t_im))
                dinv.append((v_re, v_im))
                b_all.append((b_re, b_im))
                z_first.append(cmul(i_re, i_im, spec[0, p], spec[1, p]))
                d_first.append((d_re + g_re, d_im + g_im))
            z, d = z_first, d_first
            for sweep in range(1, SWEEPS):
                zn_re = near((z[0][0], z[1][0]))
                zn_im = near((z[0][1], z[1][1]))
                dn_re = near((d[0][0], d[1][0]))
                dn_im = near((d[0][1], d[1][1]))
                z_next, d_next = [], []
                for p in range(2):
                    re, im = cmul(inv[p][0], inv[p][1], dn_re[p], dn_im[p])
                    z_next.append((z_first[p][0] - re, z_first[p][1] - im))
                    re, im = cmul(turn[p][0], turn[p][1], zn_re[p], zn_im[p])
                    d_next.append((d_first[p][0] + re, d_first[p][1] + im))
                z, d = z_next, d_next
            for p in range(2):
                grav = coef[3, p][:, 0:count]
                hb_re, hb_im = cmul(
                    b_all[p][0][:, 0:count],
                    b_all[p][1][:, 0:count],
                    spec[4, p, :, 0:count],
                    spec[5, p, :, 0:count],
                )
                nh_re = hb_re - grav * (spec[2, p, :, 0:count] + zn_re[p][:, 0:count])
                nh_im = hb_im - grav * (spec[3, p, :, 0:count] + zn_im[p][:, 0:count])
                h = cmul(nh_re, nh_im, dinv[p][0][:, 0:count], dinv[p][1][:, 0:count])
                for f, (re, im) in enumerate((z[p], d[p], h)):
                    o_re, o_im = cmul(w_re, w_im, re[:, 0:count], im[:, 0:count])
                    out_ref[2 * f, p, home, :] += o_re
                    out_ref[2 * f + 1, p, home, :] += o_im
            return carry

        lax.fori_loop(0, solves, pole_step, 0)
        return carry

    lax.fori_loop(0, groups, group_step, 0)

    for g in range(groups):

        def finish(step, carry, g=g):
            exchange(g, lax.rem(me + step, waves), me).wait_send()
            return carry

        lax.fori_loop(1, waves, finish, 0)


def shards(grid, legendre, wave_table, pole_table, pole_index):
    waves = lax.axis_size("wave")
    poles = lax.axis_size("pole")
    comps, _, lat = grid.shape
    slots, _, north, count = legendre.shape
    groups = slots // GROUP
    rows = GROUP * comps
    width = count + LANES
    f32 = jnp.float32
    return pl.pallas_call(
        functools.partial(kernel, waves, poles),
        out_shape=jax.ShapeDtypeStruct((comps, 2, slots, count), f32),
        in_specs=[
            pl.BlockSpec(memory_space=pl.ANY),
            pl.BlockSpec(memory_space=pl.ANY),
            pl.BlockSpec(memory_space=pltpu.SMEM),
            pl.BlockSpec(memory_space=pltpu.SMEM),
            pl.BlockSpec(memory_space=pltpu.SMEM),
        ],
        out_specs=pl.BlockSpec(memory_space=pltpu.VMEM),
        scratch_shapes=[
            pltpu.VMEM(grid.shape, f32),
            pltpu.VMEM(legendre.shape, jnp.bfloat16),
            pltpu.VMEM((groups, waves, rows, lat), f32),
            pltpu.VMEM((groups, waves, rows, lat), f32),
            pltpu.VMEM((waves // 2, 2, rows + 8, lat), f32),
            pltpu.VMEM((comps, 2, GROUP, width), f32),
            pltpu.VMEM((4, 2, GROUP, width), f32),
            pltpu.VMEM((groups, 2, GROUP, LANES), f32),
            pltpu.VMEM((groups, 2, GROUP, LANES), f32),
            pltpu.SemaphoreType.DMA,
            pltpu.SemaphoreType.DMA((slots,)),
            pltpu.SemaphoreType.DMA((groups, waves)),
            pltpu.SemaphoreType.DMA((groups, waves)),
            pltpu.SemaphoreType.DMA((groups, 2)),
            pltpu.SemaphoreType.DMA((groups, 2)),
        ],
        compiler_params=pltpu.CompilerParams(
            collective_id=0, has_side_effects=True, vmem_limit_bytes=48 * 1024 * 1024
        ),
    )(grid, legendre, wave_table, pole_table, pole_index)


def solution(mesh):
    in_specs = (P(None, None, "wave"), P("wave", None, None, "pole"), P(), P(), P())
    out_specs = P(None, None, "wave", "pole")
    return jax.shard_map(shards, mesh=mesh, in_specs=in_specs, out_specs=out_specs, check_vma=False)
```

```python
import functools

import jax
import jax.numpy as jnp
from jax import lax
from jax.experimental import pallas as pl
from jax.experimental.pallas import tpu as pltpu
from jax.sharding import PartitionSpec as P

SWEEPS = 8
GROUP = 8
HALO = 4
BATCH = 4
LANES = 128
MESH = pl.DeviceIdType.MESH

coriolis_step = 1.2
gravity_step = 0.0008


def cmul(are, aim, bre, bim):
    return (are * bre - aim * bim, are * bim + aim * bre)


def coefficients(wave, position, valid, parity):
    order = 2.0 * position + parity
    degree = wave + order
    product = degree * (degree + 1.0)
    rossby = coriolis_step * wave / jnp.maximum(product, 2.0)
    gravity = gravity_step * jnp.sqrt(product)
    e_lo = jnp.sqrt(order * (2.0 * wave + order) / jnp.maximum(4.0 * degree * degree - 1.0, 1.0))
    after = order + 1.0
    upper_deg = degree + 1.0
    e_hi = jnp.sqrt(
        after * (2.0 * wave + after) / jnp.maximum(4.0 * upper_deg * upper_deg - 1.0, 1.0)
    )
    e_lo = jnp.where(valid, coriolis_step * e_lo, 0.0)
    e_hi = jnp.where(valid, coriolis_step * e_hi, 0.0)
    return e_lo, e_hi, rossby, gravity


def kernel(
    waves,
    poles,
    grid_hbm,
    leg_hbm,
    wave_table,
    pole_table,
    pole_index,
    out_ref,
    grid_v,
    leg_v,
    send,
    recv,
    parts,
    spec,
    coef,
    halo_send,
    halo_recv,
    grid_sem,
    leg_sem,
    send_sem,
    recv_sem,
    halo_send_sem,
    halo_recv_sem,
):
    comps = grid_hbm.shape[0]
    lat = grid_hbm.shape[2]
    slots = leg_hbm.shape[0]
    count = leg_hbm.shape[3]
    groups = slots // GROUP
    half = waves // 2
    rows = GROUP * comps
    width = count + LANES
    solves = pole_index.shape[0]
    batch = next(b for b in (BATCH, 2, 1) if solves % b == 0)
    me = lax.axis_index("wave")
    zone = lax.axis_index("pole")

    barrier = pltpu.get_barrier_semaphore()
    for step in range(1, waves):
        pl.semaphore_signal(
            barrier, inc=1, device_id=(lax.rem(me + step, waves), zone), device_id_type=MESH
        )

    @pl.when(zone > 0)
    def _():
        pl.semaphore_signal(barrier, inc=1, device_id=(me, zone - 1), device_id_type=MESH)

    @pl.when(zone < poles - 1)
    def _():
        pl.semaphore_signal(barrier, inc=1, device_id=(me, zone + 1), device_id_type=MESH)

    grid_copy = pltpu.make_async_copy(grid_hbm, grid_v, grid_sem)
    grid_copy.start()
    leg_copies = [
        pltpu.make_async_copy(leg_hbm.at[s], leg_v.at[s], leg_sem.at[s]) for s in range(slots)
    ]
    for copy in leg_copies:
        copy.start()
    parts[:, :, rows:, :] = jnp.zeros((half, 2, parts.shape[2] - rows, lat), jnp.float32)
    grid_copy.wait()

    def collect(target, g, d):
        for s in range(GROUP):
            m = wave_table[d * slots + g * GROUP + s]
            for c in range(comps):
                target[g, d, s * comps + c : s * comps + c + 1, :] = grid_v[c, pl.ds(m, 1), :]

    def exchange(g, there, here):
        return pltpu.make_async_remote_copy(
            src_ref=send.at[g, there],
            dst_ref=recv.at[g, here],
            send_sem=send_sem.at[g, there],
            recv_sem=recv_sem.at[g, here],
            device_id=(there, zone),
            device_id_type=MESH,
        )

    neighbours = (zone > 0).astype(jnp.int32) + (zone < poles - 1).astype(jnp.int32)
    pl.semaphore_wait(barrier, waves - 1 + neighbours)

    for g in range(groups):

        def send_one(step, carry, g=g):
            there = lax.rem(me + step, waves)
            collect(send, g, there)
            exchange(g, there, me).start()
            return carry

        lax.fori_loop(1, waves, send_one, 0)
    for g in range(groups):
        collect(recv, g, me)

    lane = lax.broadcasted_iota(jnp.int32, (GROUP, LANES), 1)
    line = lax.broadcasted_iota(jnp.int32, (GROUP, width), 0)
    place = lax.broadcasted_iota(jnp.int32, (GROUP, width), 1)
    local = jnp.where(place >= width - HALO, place - width, place)
    k_index = local + zone * count
    valid = (local < count + HALO) & (k_index >= 0) & (k_index < poles * count)
    position = k_index.astype(jnp.float32)

    def left_copy(g):
        return pltpu.make_async_remote_copy(
            src_ref=halo_send.at[g, 0],
            dst_ref=halo_recv.at[g, 1],
            send_sem=halo_send_sem.at[g, 0],
            recv_sem=halo_recv_sem.at[g, 1],
            device_id=(me, lax.rem(zone + poles - 1, poles)),
            device_id_type=MESH,
        )

    def right_copy(g):
        return pltpu.make_async_remote_copy(
            src_ref=halo_send.at[g, 1],
            dst_ref=halo_recv.at[g, 0],
            send_sem=halo_send_sem.at[g, 1],
            recv_sem=halo_recv_sem.at[g, 0],
            device_id=(me, lax.rem(zone + 1, poles)),
            device_id_type=MESH,
        )

    def prepare(g, carry):
        wave = jnp.zeros((GROUP, width), jnp.float32)
        for s in range(GROUP):
            m = wave_table[me * slots + g * GROUP + s].astype(jnp.float32)
            wave = jnp.where(line == s, m, wave)
        for p in range(2):
            for i, value in enumerate(coefficients(wave, position, valid, float(p))):
                coef[g, i, p] = value
        return carry

    lax.fori_loop(0, groups, prepare, 0)

    def analyse_group(g, carry):
        for w in range(half):
            for source in (w, w + half):

                @pl.when(me != source)
                def _():
                    exchange(g, source, source).wait_recv()

            north = recv[g, w]
            south = recv[g, w + half]
            parts[w, 0, 0:rows, :] = north + south
            parts[w, 1, 0:rows, :] = north - south

        span = half if lat % LANES == 0 else 1
        for s in range(GROUP):
            slot = g * GROUP + s
            pltpu.make_async_copy(leg_hbm.at[slot], leg_v.at[slot], leg_sem.at[slot]).wait()

            for p in range(2):
                total = jnp.zeros((16, count), jnp.float32)
                for first in range(0, half, span):
                    pieces = []
                    for w in range(first, first + span):
                        value = parts[w, p, s * comps : s * comps + 8, :]
                        high = value.astype(jnp.bfloat16).astype(jnp.float32)
                        pieces.append(jnp.concatenate([high, value - high], axis=0))
                    left = jnp.concatenate(pieces, axis=1) if span > 1 else pieces[0]
                    total = total + jnp.dot(
                        left.astype(jnp.bfloat16),
                        leg_v[slot, p, first * lat : (first + span) * lat, :],
                        preferred_element_type=jnp.float32,
                    )
                both = total[0:8] + total[8:16]
                for c in range(comps):
                    spec[g, c, p, s : s + 1, 0:count] = both[c : c + 1]

        lower = jnp.zeros((GROUP, LANES), jnp.float32)
        upper = jnp.zeros((GROUP, LANES), jnp.float32)
        for i in range(2 * comps):
            c, p = i // 2, i % 2
            mine = (lane >= HALO * i) & (lane < HALO * (i + 1))
            first = spec[g, c, p, :, 0:LANES]
            last = spec[g, c, p, :, count - LANES : count]
            lower = jnp.where(mine, pltpu.roll(first, HALO * i, 1) if i else first, lower)
            upper = jnp.where(mine, pltpu.roll(last, HALO * (i + 1), 1), upper)
        halo_send[g, 0] = lower
        halo_send[g, 1] = upper

        @pl.when(zone > 0)
        def _():
            left_copy(g).start()

        @pl.when(zone < poles - 1)
        def _():
            right_copy(g).start()

        return carry

    lax.fori_loop(0, groups, analyse_group, 0)

    def solve_group(g, carry):
        @pl.when(zone > 0)
        def _():
            right_copy(g).wait_recv()
            left_copy(g).wait_send()

        @pl.when(zone < poles - 1)
        def _():
            left_copy(g).wait_recv()
            right_copy(g).wait_send()

        from_left = halo_recv[g, 0]
        from_right = halo_recv[g, 1]
        for i in range(2 * comps):
            c, p = i // 2, i % 2
            right = pltpu.roll(from_right, LANES - HALO * i, 1) if i else from_right
            left = pltpu.roll(from_left, LANES - HALO * (i + 1), 1)
            edge = jnp.where((lane < HALO) & (zone < poles - 1), right, 0.0)
            edge = jnp.where((lane >= LANES - HALO) & (zone > 0), left, edge)
            spec[g, c, p, :, count:width] = edge

        home = pl.ds(pl.multiple_of(g * GROUP, GROUP), GROUP)
        out_ref[:, :, home, :] = jnp.zeros((comps, 2, GROUP, count), jnp.float32)

        def near(even, odd):
            first = coef[g, 0, 0] * pltpu.roll(odd, 1, 1) + coef[g, 1, 0] * odd
            second = coef[g, 0, 1] * even + coef[g, 1, 1] * pltpu.roll(even, width - 1, 1)
            return first, second

        def setup(a_re, a_im):
            inv, turn, z_first, d_first = [], [], [], []
            for p in range(2):
                v_re, v_im, b_re, b_im = divisor(a_re, a_im, p, width)
                grav = coef[g, 3, p]
                b_mag = 1.0 / (b_re * b_re + b_im * b_im)
                i_re, i_im = b_re * b_mag, -b_im * b_mag
                t_re, t_im = cmul(a_re, a_im, v_re, v_im)
                g_re, g_im = cmul(v_re, v_im, grav * spec[g, 4, p], grav * spec[g, 5, p])
                d_re, d_im = cmul(t_re, t_im, spec[g, 2, p], spec[g, 3, p])
                inv.append((i_re, i_im))
                turn.append((t_re, t_im))
                z_first.append(cmul(i_re, i_im, spec[g, 0, p], spec[g, 1, p]))
                d_first.append((d_re + g_re, d_im + g_im))
            return inv, turn, z_first, d_first

        def divisor(a_re, a_im, p, upto):
            rossby, grav = coef[g, 2, p, :, 0:upto], coef[g, 3, p, :, 0:upto]
            b_re = a_re + 0.0 * rossby
            b_im = a_im + rossby
            det_re, det_im = cmul(b_re, b_im, a_re, a_im)
            det_re = det_re + grav * grav
            det_mag = 1.0 / (det_re * det_re + det_im * det_im)
            return det_re * det_mag, -det_im * det_mag, b_re, b_im

        def pole_step(q, carry):
            chosen = [pole_index[q * batch + i] for i in range(batch)]
            pole = [[pole_table[r, column] for r in range(4)] for column in chosen]
            fixed = [setup(pole[i][0], pole[i][1]) for i in range(batch)]
            z = [fixed[i][2] for i in range(batch)]
            d = [fixed[i][3] for i in range(batch)]
            zn = [None] * batch
            for sweep in range(1, SWEEPS):
                for i in range(batch):
                    inv, turn, z_first, d_first = fixed[i]
                    zn_re = near(z[i][0][0], z[i][1][0])
                    zn_im = near(z[i][0][1], z[i][1][1])
                    dn_re = near(d[i][0][0], d[i][1][0])
                    dn_im = near(d[i][0][1], d[i][1][1])
                    z_next, d_next = [], []
                    for p in range(2):
                        re, im = cmul(inv[p][0], inv[p][1], dn_re[p], dn_im[p])
                        z_next.append((z_first[p][0] - re, z_first[p][1] - im))
                        re, im = cmul(turn[p][0], turn[p][1], zn_re[p], zn_im[p])
                        d_next.append((d_first[p][0] + re, d_first[p][1] + im))
                    z[i], d[i] = z_next, d_next
                    zn[i] = (zn_re, zn_im)
            for p in range(2):
                grav = coef[g, 3, p, :, 0:count]
                sums = [None] * 6
                for i in range(batch):
                    a_re, a_im, w_re, w_im = pole[i]
                    v_re, v_im, b_re, b_im = divisor(a_re, a_im, p, count)
                    hb_re, hb_im = cmul(
                        b_re, b_im, spec[g, 4, p, :, 0:count], spec[g, 5, p, :, 0:count]
                    )
                    rd_re = spec[g, 2, p, :, 0:count] + zn[i][0][p][:, 0:count]
                    rd_im = spec[g, 3, p, :, 0:count] + zn[i][1][p][:, 0:count]
                    h = cmul(hb_re - grav * rd_re, hb_im - grav * rd_im, v_re, v_im)
                    for f, (re, im) in enumerate((z[i][p], d[i][p], h)):
                        term = cmul(w_re, w_im, re[:, 0:count], im[:, 0:count])
                        for part in range(2):
                            n = 2 * f + part
                            sums[n] = term[part] if i == 0 else sums[n] + term[part]
                for n in range(6):
                    out_ref[n, p, home, :] += sums[n]
            return carry

        lax.fori_loop(0, solves // batch, pole_step, 0)
        return carry

    lax.fori_loop(0, groups, solve_group, 0)

    for g in range(groups):

        def finish(step, carry, g=g):
            exchange(g, lax.rem(me + step, waves), me).wait_send()
            return carry

        lax.fori_loop(1, waves, finish, 0)


def shards(grid, legendre, wave_table, pole_table, pole_index):
    waves = lax.axis_size("wave")
    poles = lax.axis_size("pole")
    comps, _, lat = grid.shape
    slots, _, north, count = legendre.shape
    groups = slots // GROUP
    rows = GROUP * comps
    width = count + LANES
    f32 = jnp.float32
    return pl.pallas_call(
        functools.partial(kernel, waves, poles),
        out_shape=jax.ShapeDtypeStruct((comps, 2, slots, count), f32),
        in_specs=[
            pl.BlockSpec(memory_space=pl.ANY),
            pl.BlockSpec(memory_space=pl.ANY),
            pl.BlockSpec(memory_space=pltpu.SMEM),
            pl.BlockSpec(memory_space=pltpu.SMEM),
            pl.BlockSpec(memory_space=pltpu.SMEM),
        ],
        out_specs=pl.BlockSpec(memory_space=pltpu.VMEM),
        scratch_shapes=[
            pltpu.VMEM(grid.shape, f32),
            pltpu.VMEM(legendre.shape, jnp.bfloat16),
            pltpu.VMEM((groups, waves, rows, lat), f32),
            pltpu.VMEM((groups, waves, rows, lat), f32),
            pltpu.VMEM((waves // 2, 2, rows + 8, lat), f32),
            pltpu.VMEM((groups, comps, 2, GROUP, width), f32),
            pltpu.VMEM((groups, 4, 2, GROUP, width), f32),
            pltpu.VMEM((groups, 2, GROUP, LANES), f32),
            pltpu.VMEM((groups, 2, GROUP, LANES), f32),
            pltpu.SemaphoreType.DMA,
            pltpu.SemaphoreType.DMA((slots,)),
            pltpu.SemaphoreType.DMA((groups, waves)),
            pltpu.SemaphoreType.DMA((groups, waves)),
            pltpu.SemaphoreType.DMA((groups, 2)),
            pltpu.SemaphoreType.DMA((groups, 2)),
        ],
        compiler_params=pltpu.CompilerParams(
            collective_id=0, has_side_effects=True, vmem_limit_bytes=64 * 1024 * 1024
        ),
    )(grid, legendre, wave_table, pole_table, pole_index)


def solution(mesh):
    in_specs = (P(None, None, "wave"), P("wave", None, None, "pole"), P(), P(), P())
    out_specs = P(None, None, "wave", "pole")
    return jax.shard_map(shards, mesh=mesh, in_specs=in_specs, out_specs=out_specs, check_vma=False)
```

```python
import functools

import jax
import jax.numpy as jnp
from jax import lax
from jax.experimental import pallas as pl
from jax.experimental.pallas import tpu as pltpu
from jax.sharding import PartitionSpec as P

SWEEPS = 8
GROUP = 8
HALO = 4
BATCH = 4
LANES = 128
MESH = pl.DeviceIdType.MESH

coriolis_step = 1.2
gravity_step = 0.0008


def cmul(are, aim, bre, bim):
    return (are * bre - aim * bim, are * bim + aim * bre)


def coefficients(wave, position, valid, parity):
    order = 2.0 * position + parity
    degree = wave + order
    product = degree * (degree + 1.0)
    rossby = coriolis_step * wave / jnp.maximum(product, 2.0)
    gravity = gravity_step * jnp.sqrt(product)
    e_lo = jnp.sqrt(order * (2.0 * wave + order) / jnp.maximum(4.0 * degree * degree - 1.0, 1.0))
    after = order + 1.0
    upper_deg = degree + 1.0
    e_hi = jnp.sqrt(
        after * (2.0 * wave + after) / jnp.maximum(4.0 * upper_deg * upper_deg - 1.0, 1.0)
    )
    e_lo = jnp.where(valid, coriolis_step * e_lo, 0.0)
    e_hi = jnp.where(valid, coriolis_step * e_hi, 0.0)
    return e_lo, e_hi, rossby, gravity


def kernel(
    waves,
    poles,
    grid_hbm,
    leg_hbm,
    wave_table,
    spec,
    grid_v,
    leg_v,
    send,
    recv,
    parts,
    halo_send,
    halo_recv,
    grid_sem,
    leg_sem,
    send_sem,
    recv_sem,
    halo_send_sem,
    halo_recv_sem,
):
    comps = grid_hbm.shape[0]
    lat = grid_hbm.shape[2]
    slots = leg_hbm.shape[0]
    count = leg_hbm.shape[3]
    groups = slots // GROUP
    half = waves // 2
    rows = GROUP * comps
    width = count + LANES
    me = lax.axis_index("wave")
    zone = lax.axis_index("pole")

    barrier = pltpu.get_barrier_semaphore()
    for step in range(1, waves):
        pl.semaphore_signal(
            barrier, inc=1, device_id=(lax.rem(me + step, waves), zone), device_id_type=MESH
        )

    @pl.when(zone > 0)
    def _():
        pl.semaphore_signal(barrier, inc=1, device_id=(me, zone - 1), device_id_type=MESH)

    @pl.when(zone < poles - 1)
    def _():
        pl.semaphore_signal(barrier, inc=1, device_id=(me, zone + 1), device_id_type=MESH)

    grid_copy = pltpu.make_async_copy(grid_hbm, grid_v, grid_sem)
    grid_copy.start()
    leg_copies = [
        pltpu.make_async_copy(leg_hbm.at[s], leg_v.at[s], leg_sem.at[s]) for s in range(slots)
    ]
    for copy in leg_copies:
        copy.start()
    parts[:, :, rows:, :] = jnp.zeros((half, 2, parts.shape[2] - rows, lat), jnp.float32)
    grid_copy.wait()

    def collect(target, g, d):
        for s in range(GROUP):
            m = wave_table[d * slots + g * GROUP + s]
            for c in range(comps):
                target[g, d, s * comps + c : s * comps + c + 1, :] = grid_v[c, pl.ds(m, 1), :]

    def exchange(g, there, here):
        return pltpu.make_async_remote_copy(
            src_ref=send.at[g, there],
            dst_ref=recv.at[g, here],
            send_sem=send_sem.at[g, there],
            recv_sem=recv_sem.at[g, here],
            device_id=(there, zone),
            device_id_type=MESH,
        )

    neighbours = (zone > 0).astype(jnp.int32) + (zone < poles - 1).astype(jnp.int32)
    pl.semaphore_wait(barrier, waves - 1 + neighbours)

    for g in range(groups):

        def send_one(step, carry, g=g):
            there = lax.rem(me + step, waves)
            collect(send, g, there)
            exchange(g, there, me).start()
            return carry

        lax.fori_loop(1, waves, send_one, 0)
    for g in range(groups):
        collect(recv, g, me)

    lane = lax.broadcasted_iota(jnp.int32, (GROUP, LANES), 1)
    def left_copy(g):
        return pltpu.make_async_remote_copy(
            src_ref=halo_send.at[g, 0],
            dst_ref=halo_recv.at[g, 1],
            send_sem=halo_send_sem.at[g, 0],
            recv_sem=halo_recv_sem.at[g, 1],
            device_id=(me, lax.rem(zone + poles - 1, poles)),
            device_id_type=MESH,
        )

    def right_copy(g):
        return pltpu.make_async_remote_copy(
            src_ref=halo_send.at[g, 1],
            dst_ref=halo_recv.at[g, 0],
            send_sem=halo_send_sem.at[g, 1],
            recv_sem=halo_recv_sem.at[g, 0],
            device_id=(me, lax.rem(zone + 1, poles)),
            device_id_type=MESH,
        )

    def analyse_group(g, carry):
        for w in range(half):
            for source in (w, w + half):

                @pl.when(me != source)
                def _():
                    exchange(g, source, source).wait_recv()

            north = recv[g, w]
            south = recv[g, w + half]
            parts[w, 0, 0:rows, :] = north + south
            parts[w, 1, 0:rows, :] = north - south

        span = half if lat % LANES == 0 else 1
        for s in range(GROUP):
            slot = g * GROUP + s
            pltpu.make_async_copy(leg_hbm.at[slot], leg_v.at[slot], leg_sem.at[slot]).wait()

            for p in range(2):
                total = jnp.zeros((16, count), jnp.float32)
                for first in range(0, half, span):
                    pieces = []
                    for w in range(first, first + span):
                        value = parts[w, p, s * comps : s * comps + 8, :]
                        high = value.astype(jnp.bfloat16).astype(jnp.float32)
                        pieces.append(jnp.concatenate([high, value - high], axis=0))
                    left = jnp.concatenate(pieces, axis=1) if span > 1 else pieces[0]
                    total = total + jnp.dot(
                        left.astype(jnp.bfloat16),
                        leg_v[slot, p, first * lat : (first + span) * lat, :],
                        preferred_element_type=jnp.float32,
                    )
                both = total[0:8] + total[8:16]
                for c in range(comps):
                    spec[g, c, p, s : s + 1, 0:count] = both[c : c + 1]

        lower = jnp.zeros((GROUP, LANES), jnp.float32)
        upper = jnp.zeros((GROUP, LANES), jnp.float32)
        for i in range(2 * comps):
            c, p = i // 2, i % 2
            mine = (lane >= HALO * i) & (lane < HALO * (i + 1))
            first = spec[g, c, p, :, 0:LANES]
            last = spec[g, c, p, :, count - LANES : count]
            lower = jnp.where(mine, pltpu.roll(first, HALO * i, 1) if i else first, lower)
            upper = jnp.where(mine, pltpu.roll(last, HALO * (i + 1), 1), upper)
        halo_send[g, 0] = lower
        halo_send[g, 1] = upper

        @pl.when(zone > 0)
        def _():
            left_copy(g).start()

        @pl.when(zone < poles - 1)
        def _():
            right_copy(g).start()

        return carry

    lax.fori_loop(0, groups, analyse_group, 0)

    def place_halo(g, carry):
        @pl.when(zone > 0)
        def _():
            right_copy(g).wait_recv()
            left_copy(g).wait_send()

        @pl.when(zone < poles - 1)
        def _():
            left_copy(g).wait_recv()
            right_copy(g).wait_send()

        from_left = halo_recv[g, 0]
        from_right = halo_recv[g, 1]
        for i in range(2 * comps):
            c, p = i // 2, i % 2
            right = pltpu.roll(from_right, LANES - HALO * i, 1) if i else from_right
            left = pltpu.roll(from_left, LANES - HALO * (i + 1), 1)
            edge = jnp.where((lane < HALO) & (zone < poles - 1), right, 0.0)
            edge = jnp.where((lane >= LANES - HALO) & (zone > 0), left, edge)
            spec[g, c, p, :, count:width] = edge

        return carry

    lax.fori_loop(0, groups, place_halo, 0)

    for g in range(groups):

        def finish(step, carry, g=g):
            exchange(g, lax.rem(me + step, waves), me).wait_send()
            return carry

        lax.fori_loop(1, waves, finish, 0)


def solve_kernel(poles, spec, wave_table, pole_table, pole_index, out_ref, coef):
    groups, comps, _, _, width = spec.shape
    count = width - LANES
    slots = groups * GROUP
    solves = pole_index.shape[0]
    batch = next(b for b in (BATCH, 2, 1) if solves % b == 0)
    me = lax.axis_index("wave")
    zone = lax.axis_index("pole")
    line = lax.broadcasted_iota(jnp.int32, (GROUP, width), 0)
    place = lax.broadcasted_iota(jnp.int32, (GROUP, width), 1)
    local = jnp.where(place >= width - HALO, place - width, place)
    k_index = local + zone * count
    valid = (local < count + HALO) & (k_index >= 0) & (k_index < poles * count)
    position = k_index.astype(jnp.float32)

    def prepare(g, carry):
        wave = jnp.zeros((GROUP, width), jnp.float32)
        for s in range(GROUP):
            m = wave_table[me * slots + g * GROUP + s].astype(jnp.float32)
            wave = jnp.where(line == s, m, wave)
        for p in range(2):
            for i, value in enumerate(coefficients(wave, position, valid, float(p))):
                coef[g, i, p] = value
        return carry

    lax.fori_loop(0, groups, prepare, 0)

    def solve_group(g, carry):
        home = pl.ds(pl.multiple_of(g * GROUP, GROUP), GROUP)
        out_ref[:, :, home, :] = jnp.zeros((comps, 2, GROUP, count), jnp.float32)

        def near(even, odd):
            first = coef[g, 0, 0] * pltpu.roll(odd, 1, 1) + coef[g, 1, 0] * odd
            second = coef[g, 0, 1] * even + coef[g, 1, 1] * pltpu.roll(even, width - 1, 1)
            return first, second

        def setup(a_re, a_im):
            inv, turn, z_first, d_first = [], [], [], []
            for p in range(2):
                v_re, v_im, b_re, b_im = divisor(a_re, a_im, p, width)
                grav = coef[g, 3, p]
                b_mag = 1.0 / (b_re * b_re + b_im * b_im)
                i_re, i_im = b_re * b_mag, -b_im * b_mag
                t_re, t_im = cmul(a_re, a_im, v_re, v_im)
                g_re, g_im = cmul(v_re, v_im, grav * spec[g, 4, p], grav * spec[g, 5, p])
                d_re, d_im = cmul(t_re, t_im, spec[g, 2, p], spec[g, 3, p])
                inv.append((i_re, i_im))
                turn.append((t_re, t_im))
                z_first.append(cmul(i_re, i_im, spec[g, 0, p], spec[g, 1, p]))
                d_first.append((d_re + g_re, d_im + g_im))
            return inv, turn, z_first, d_first

        def divisor(a_re, a_im, p, upto):
            rossby, grav = coef[g, 2, p, :, 0:upto], coef[g, 3, p, :, 0:upto]
            b_re = a_re + 0.0 * rossby
            b_im = a_im + rossby
            det_re, det_im = cmul(b_re, b_im, a_re, a_im)
            det_re = det_re + grav * grav
            det_mag = 1.0 / (det_re * det_re + det_im * det_im)
            return det_re * det_mag, -det_im * det_mag, b_re, b_im

        def pole_step(q, carry):
            chosen = [pole_index[q * batch + i] for i in range(batch)]
            pole = [[pole_table[r, column] for r in range(4)] for column in chosen]
            fixed = [setup(pole[i][0], pole[i][1]) for i in range(batch)]
            z = [fixed[i][2] for i in range(batch)]
            d = [fixed[i][3] for i in range(batch)]
            zn = [None] * batch
            for sweep in range(1, SWEEPS):
                for i in range(batch):
                    inv, turn, z_first, d_first = fixed[i]
                    zn_re = near(z[i][0][0], z[i][1][0])
                    zn_im = near(z[i][0][1], z[i][1][1])
                    dn_re = near(d[i][0][0], d[i][1][0])
                    dn_im = near(d[i][0][1], d[i][1][1])
                    z_next, d_next = [], []
                    for p in range(2):
                        re, im = cmul(inv[p][0], inv[p][1], dn_re[p], dn_im[p])
                        z_next.append((z_first[p][0] - re, z_first[p][1] - im))
                        re, im = cmul(turn[p][0], turn[p][1], zn_re[p], zn_im[p])
                        d_next.append((d_first[p][0] + re, d_first[p][1] + im))
                    z[i], d[i] = z_next, d_next
                    zn[i] = (zn_re, zn_im)
            for p in range(2):
                grav = coef[g, 3, p, :, 0:count]
                sums = [None] * 6
                for i in range(batch):
                    a_re, a_im, w_re, w_im = pole[i]
                    v_re, v_im, b_re, b_im = divisor(a_re, a_im, p, count)
                    hb_re, hb_im = cmul(
                        b_re, b_im, spec[g, 4, p, :, 0:count], spec[g, 5, p, :, 0:count]
                    )
                    rd_re = spec[g, 2, p, :, 0:count] + zn[i][0][p][:, 0:count]
                    rd_im = spec[g, 3, p, :, 0:count] + zn[i][1][p][:, 0:count]
                    h = cmul(hb_re - grav * rd_re, hb_im - grav * rd_im, v_re, v_im)
                    for f, (re, im) in enumerate((z[i][p], d[i][p], h)):
                        term = cmul(w_re, w_im, re[:, 0:count], im[:, 0:count])
                        for part in range(2):
                            n = 2 * f + part
                            sums[n] = term[part] if i == 0 else sums[n] + term[part]
                for n in range(6):
                    out_ref[n, p, home, :] += sums[n]
            return carry

        lax.fori_loop(0, solves // batch, pole_step, 0)
        return carry

    lax.fori_loop(0, groups, solve_group, 0)


def shards(grid, legendre, wave_table, pole_table, pole_index):
    waves = lax.axis_size("wave")
    poles = lax.axis_size("pole")
    comps, _, lat = grid.shape
    slots, _, north, count = legendre.shape
    groups = slots // GROUP
    rows = GROUP * comps
    width = count + LANES
    f32 = jnp.float32
    anywhere = pl.BlockSpec(memory_space=pl.ANY)
    scalars = pl.BlockSpec(memory_space=pltpu.SMEM)
    vector = pl.BlockSpec(memory_space=pltpu.VMEM)
    spec = pl.pallas_call(
        functools.partial(kernel, waves, poles),
        out_shape=jax.ShapeDtypeStruct((groups, comps, 2, GROUP, width), f32),
        in_specs=[anywhere, anywhere, scalars],
        out_specs=vector,
        scratch_shapes=[
            pltpu.VMEM(grid.shape, f32),
            pltpu.VMEM(legendre.shape, jnp.bfloat16),
            pltpu.VMEM((groups, waves, rows, lat), f32),
            pltpu.VMEM((groups, waves, rows, lat), f32),
            pltpu.VMEM((waves // 2, 2, rows + 8, lat), f32),
            pltpu.VMEM((groups, 2, GROUP, LANES), f32),
            pltpu.VMEM((groups, 2, GROUP, LANES), f32),
            pltpu.SemaphoreType.DMA,
            pltpu.SemaphoreType.DMA((slots,)),
            pltpu.SemaphoreType.DMA((groups, waves)),
            pltpu.SemaphoreType.DMA((groups, waves)),
            pltpu.SemaphoreType.DMA((groups, 2)),
            pltpu.SemaphoreType.DMA((groups, 2)),
        ],
        compiler_params=pltpu.CompilerParams(
            collective_id=0, has_side_effects=True, vmem_limit_bytes=64 * 1024 * 1024
        ),
    )(grid, legendre, wave_table)
    return pl.pallas_call(
        functools.partial(solve_kernel, poles),
        out_shape=jax.ShapeDtypeStruct((comps, 2, slots, count), f32),
        in_specs=[vector, scalars, scalars, scalars],
        out_specs=vector,
        scratch_shapes=[pltpu.VMEM((groups, 4, 2, GROUP, width), f32)],
        compiler_params=pltpu.CompilerParams(vmem_limit_bytes=64 * 1024 * 1024),
    )(spec, wave_table, pole_table, pole_index)


def solution(mesh):
    in_specs = (P(None, None, "wave"), P("wave", None, None, "pole"), P(), P(), P())
    out_specs = P(None, None, "wave", "pole")
    return jax.shard_map(shards, mesh=mesh, in_specs=in_specs, out_specs=out_specs, check_vma=False)
```
